32 devices in a mesh: groups: 2 (over y), train: 4 (over x, core), proj: 4 (over z).
Axes of the slice: x: 2, y: 2, z: 4, core: 2. Of those that a mesh axis runs over, the one named last changes fastest.
Arguments:
- train_grads: bfloat16 [8192, 16384], P(('groups', 'train'), 'proj'), parts along dimension 0, may hold values from -6 to 6
- queries: bfloat16 [4096, 16384], P(('groups', 'train'), 'proj'), parts along dimension 0, may hold values from -6 to 6
- fisher: float32 [32768], P(('groups', 'proj')), parts along dimension 0, may hold values from 0.25 to 4
- block_pick: int32 [8, 4], P('groups'), parts along dimension 0, may hold values from 0 to 1
Outputs:
- scores: float32 [4, 8192, 256], P(None, ('groups', 'train', 'proj')), parts along dimension 1
The draws below stay inside these ranges and needn't reach their ends.
There are 2 independent parts, one for each index of `groups`. The reference program is written for one: setup_inputs(seed, part) draws one part's arguments, and reference() takes and returns one part's arrays. A program takes and returns all parts, laid end to end along the dimension named above; each array names one. Nothing has to cross between parts.
All inputs are finite; a program needn't handle non-finite values.
Results may differ from the reference program's by a relative error of at most 0.0029.
Values may be sent and summed in bfloat16 or wider, within the bound.
A program may use at most 128 MiB of HBM per device.

```python
import math
import jax
import jax.numpy as jnp
from jax import lax

P_SIZE = 16384
QB = 256
QBLK = 2
STEPS = 4
ROWS = 1024
NTR = 4096
NQ = 2048
N_TRAIN = 4


def plant(result, rng, low, high):
    spot = [jax.random.randint(jax.random.fold_in(rng, axis), (), 0, length) for axis, length in enumerate(result.shape)]
    longest = result.shape.index(max(result.shape))
    beside = spot[:longest] + [(spot[longest] + 1) % result.shape[longest]] + spot[longest + 1:]
    return result.at[tuple(spot)].set(low).at[tuple(beside)].set(high)


def level_of(own_key, dims, shards, smallest, high):
    gain, own = 1.0, jax.random.fold_in(own_key, 6)
    for axis_at, blocks in shards:
        draws = jnp.exp(jax.random.uniform(jax.random.fold_in(own, axis_at), (blocks,), jnp.float32, smallest / len(shards), high / len(shards)))
        gain = gain * jnp.repeat(draws, dims[axis_at] // blocks).reshape([-1 if axis == axis_at else 1 for axis in range(len(dims))])
    return gain


def centred(rng, shape, deviation, most, split=(), kind=jnp.bfloat16):
    drawn = jax.random.normal(rng, shape, jnp.float32) * deviation
    if len(split) > 0:
        drawn = level_of(rng, shape, split, -0.22, 0.18) * drawn
    return jnp.clip(drawn, min=-most, max=most).astype(kind)


def setup_inputs(seed: int = 0, part: int = 0) -> dict:
    splits = jax.random.split(jax.random.key(seed), 5)
    part_splits = jax.random.split(jax.random.fold_in(splits[4], part), 5)
    train_grads = centred(part_splits[0], (NTR, P_SIZE), 1.0, 6.0, ((0, 4), (1, 4)))
    queries = centred(part_splits[1], (NQ, P_SIZE), 1.0, 6.0, ((0, 4), (1, 4)))
    fisher = jnp.clip(jnp.exp(math.log(4.0) - 2.7725887 * jax.random.uniform(part_splits[2], (P_SIZE,), jnp.float32) ** level_of(part_splits[2], (P_SIZE,), ((0, 4),), -0.2, 0.2)), 0.25, 4.0)
    block_pick = plant(jax.random.randint(part_splits[3], (STEPS, N_TRAIN), 0, QBLK), jax.random.fold_in(part_splits[3], 1), 0, QBLK - 1).astype(jnp.int32)
    return {"train_grads": train_grads, "queries": queries, "fisher": fisher, "block_pick": block_pick}


def reference(train_grads, queries, fisher, block_pick):
    precond = (queries.astype(jnp.float32) * lax.rsqrt(fisher)[None, :]).astype(jnp.bfloat16)
    blocks = precond.reshape(N_TRAIN, QBLK, QB, P_SIZE)
    grads = train_grads.reshape(N_TRAIN, ROWS, P_SIZE)
    owners = jnp.arange(N_TRAIN, dtype=jnp.int32)

    def device_tiles(operands):
        left = operands[0].astype(jnp.float32)
        right = operands[1].astype(jnp.float32)
        return jnp.dot(left, right.T, precision=lax.Precision.HIGHEST)
    results = []
    for step in range(STEPS):
        sources = (owners - step) % N_TRAIN
        chosen = blocks[sources, block_pick[step, sources]]
        tiles = lax.map(device_tiles, (grads, chosen))
        results.append(tiles.reshape(N_TRAIN * ROWS, QB) * P_SIZE ** (-0.5))
    return jnp.stack(results)
```

```python
import functools

import jax
import jax.numpy as jnp
from jax import lax
from jax.experimental import pallas as pl
from jax.experimental.pallas import tpu as pltpu
from jax.sharding import PartitionSpec as P

P_SIZE = 16384
QB = 256
QBLK = 2
STEPS = 4
CHUNK = 64
NCHUNK = QB // CHUNK
MESH = pl.DeviceIdType.MESH


def kernel(
    n_train, n_proj, train_hbm, pool_hbm, fisher, pick, out,
    train, pools, inv_root, outgoing, block, partial, own, landed,
    train_sem, pool_sem, send_sem, recv_sem, zsend_sem, zrecv_sem,
):
    here, z = lax.axis_index("train"), lax.axis_index("proj")
    core = lax.rem(here, 2)
    rows, width = train.shape
    owned = rows // n_proj
    scale = P_SIZE ** (-0.5)

    pool_copies = []
    for c in range(NCHUNK):
        part = pl.ds(c * CHUNK, CHUNK)
        copy = pltpu.make_async_copy(pool_hbm.at[:, part], pools[c], pool_sem.at[c])
        copy.start()
        pool_copies.append(copy)
    train_copy = pltpu.make_async_copy(train_hbm, train, train_sem)
    train_copy.start()

    barrier = pltpu.get_barrier_semaphore()
    for step in range(1, STEPS):
        source = lax.rem(here - step + n_train, n_train)
        pl.semaphore_signal(barrier, inc=1, device_id={"train": source}, device_id_type=MESH)
    for d in range(1, n_proj):
        pl.semaphore_signal(
            barrier, inc=1, device_id={"proj": lax.rem(z - d + n_proj, n_proj)}, device_id_type=MESH
        )
    inv_root[...] = lax.rsqrt(fisher[...])

    def query_copy(step, c):
        part = pl.ds(c * CHUNK, CHUNK)
        return pltpu.make_async_remote_copy(
            src_ref=outgoing.at[step - 1, part],
            dst_ref=block.at[step, part],
            send_sem=send_sem.at[step - 1, c],
            recv_sem=recv_sem.at[step - 1, c],
            device_id={"train": lax.rem(here + step, n_train)},
            device_id_type=MESH,
        )

    def condition(step, c, target, slot):
        chosen = pick[step, here]
        piece = min(width, 512)

        def body(i, _):
            source = pl.ds(pl.multiple_of(i * 16, 16), 16)
            part = pl.ds(pl.multiple_of(c * CHUNK + i * 16, 16), 16)
            for at in range(0, width, piece):
                lanes = pl.ds(at, piece)
                value = pools[c][chosen, source, lanes].astype(jnp.float32) * inv_root[:, lanes]
                target[slot, part, lanes] = value.astype(jnp.bfloat16)
            return 0

        lax.fori_loop(0, CHUNK // 16, body, 0)

    far = (2 - core, 3 - core)
    near = 1 + 2 * core
    for c in range(NCHUNK):
        pool_copies[c].wait()
        for i, step in enumerate((*far, near)):
            condition(step, c, outgoing, step - 1)
            if c == 0 and i == 0:
                pl.semaphore_wait(barrier, STEPS - 1 + n_proj - 1)
            query_copy(step, c).start()
    for c in range(NCHUNK):
        condition(0, c, block, 0)
    train_copy.wait()

    def partial_copy(k, d):
        to = lax.rem(z + d, n_proj)
        return pltpu.make_async_remote_copy(
            src_ref=partial.at[k, pl.ds(pl.multiple_of(to * owned, 16), owned)],
            dst_ref=landed.at[k, d - 1],
            send_sem=zsend_sem.at[k, d - 1],
            recv_sem=zrecv_sem.at[k, d - 1],
            device_id={"proj": to},
            device_id_type=MESH,
        )

    def finish(k, streams, c):
        def add(d, total):
            partial_copy(k, d).wait_recv()
            return total + landed[k, d - 1].astype(jnp.float32)

        total = lax.fori_loop(1, n_proj, add, own[k]) * scale
        for i, step in enumerate(streams):
            out[step, :, c * CHUNK:(c + 1) * CHUNK] = total[:, i * CHUNK:(i + 1) * CHUNK]

    near_in = 3 - 2 * core
    far_in = (1 + core, 2 + core)
    work = [((0, near_in), c) for c in range(NCHUNK)] + [(far_in, c) for c in range(NCHUNK)]
    for k, (streams, c) in enumerate(work):
        part = slice(c * CHUNK, (c + 1) * CHUNK)
        for step in streams:
            if not (isinstance(step, int) and step == 0):
                query_copy(step, c).wait_recv()

        def multiply(d, _):
            to = lax.rem(z + d, n_proj)
            mine = pl.ds(pl.multiple_of(to * owned, 16), owned)
            both = jnp.concatenate([block[step, part] for step in streams], axis=0)
            sums = lax.dot_general(
                train[mine], both, (((1,), (1,)), ((), ())), preferred_element_type=jnp.float32
            )

            @pl.when(d < n_proj)
            def _():
                partial[k, mine] = sums.astype(jnp.bfloat16)
                partial_copy(k, d).start()

            @pl.when(d == n_proj)
            def _():
                own[k] = sums

            return 0

        lax.fori_loop(1, n_proj + 1, multiply, 0)
        if k > 0:
            finish(k - 1, *work[k - 1])
    finish(len(work) - 1, *work[-1])

    for step in range(1, STEPS):
        for c in range(NCHUNK):
            query_copy(step, c).wait_send()
    for k in range(len(work)):
        def drain(d, _):
            partial_copy(k, d).wait_send()
            return 0

        lax.fori_loop(1, n_proj, drain, 0)


def on_device(n_train, n_proj, train_grads, queries, fisher, block_pick):
    rows, width = train_grads.shape
    owned = rows // n_proj
    works = 2 * NCHUNK
    bf16, f32 = jnp.bfloat16, jnp.float32
    dma = pltpu.SemaphoreType.DMA
    return pl.pallas_call(
        functools.partial(kernel, n_train, n_proj),
        out_shape=jax.ShapeDtypeStruct((STEPS, owned, QB), f32),
        in_specs=[
            pl.BlockSpec(memory_space=pl.ANY),
            pl.BlockSpec(memory_space=pl.ANY),
            pl.BlockSpec(memory_space=pltpu.VMEM),
            pl.BlockSpec(memory_space=pltpu.SMEM),
        ],
        out_specs=pl.BlockSpec(memory_space=pltpu.VMEM),
        scratch_shapes=[
            pltpu.VMEM((rows, width), bf16),
            [pltpu.VMEM((QBLK, CHUNK, width), bf16)] * NCHUNK,
            pltpu.VMEM((1, width), f32),
            pltpu.VMEM((STEPS - 1, QB, width), bf16),
            pltpu.VMEM((STEPS, QB, width), bf16),
            pltpu.VMEM((works, rows, 2 * CHUNK), bf16),
            pltpu.VMEM((works, owned, 2 * CHUNK), f32),
            pltpu.VMEM((works, n_proj - 1, owned, 2 * CHUNK), bf16),
            dma(()),
            dma((NCHUNK,)),
            dma((STEPS - 1, NCHUNK)),
            dma((STEPS - 1, NCHUNK)),
            dma((works, n_proj - 1)),
            dma((works, n_proj - 1)),
        ],
        compiler_params=pltpu.CompilerParams(
            collective_id=0, has_side_effects=True, vmem_limit_bytes=50 * 1024 * 1024
        ),
        cost_estimate=pl.CostEstimate(
            flops=2 * STEPS * rows * width * QB, bytes_accessed=2 * width * (rows + 512), transcendentals=width
        ),
    )(train_grads, queries.reshape(QBLK, QB, width), fisher.reshape(1, width), block_pick)


def solution(mesh):
    placed = (
        P(("groups", "train"), "proj"),
        P(("groups", "train"), "proj"),
        P(("groups", "proj")),
        P("groups", None),
    )
    return jax.shard_map(
        functools.partial(on_device, mesh.shape["train"], mesh.shape["proj"]),
        mesh=mesh,
        in_specs=placed,
        out_specs=P(None, ("groups", "train", "proj"), None),
        check_vma=False,
    )
```

```python
import functools

import jax
import jax.numpy as jnp
from jax import lax
from jax.experimental import pallas as pl
from jax.experimental.pallas import tpu as pltpu
from jax.sharding import PartitionSpec as P

P_SIZE = 16384
QB = 256
QBLK = 2
STEPS = 4
LANES = 128
CHUNK = 64
NCHUNK = QB // CHUNK
FAR_ROWS = (32, 32, 64, 64, 32, 16, 16)
FAR_AT = tuple(sum(FAR_ROWS[:i]) for i in range(len(FAR_ROWS)))
FAR_CUTS = (1,) * (len(FAR_ROWS) - 1) + (2,)
NFAR = len(FAR_ROWS)
MAX_CUTS = max(FAR_CUTS)
MESH = pl.DeviceIdType.MESH


def fold_of(count):
    return LANES // (2 * count)


def kernel(
    n_train, n_proj, train_hbm, pool_hbm, fisher_hbm, pick_hbm, out,
    train, pools, fisher, inv_root, pick, far_out, near_out, near_blocks, far_blocks,
    partials, owns, landed, early,
    train_sem, pool_sem, small_sem, fsend_sem, frecv_sem, nsend_sem, nrecv_sem, zsend_sem, zrecv_sem,
):
    here, z = lax.axis_index("train"), lax.axis_index("proj")
    core = lax.rem(here, 2)
    rows, width = train.shape
    owned = rows // n_proj
    scale = P_SIZE ** (-0.5)

    barrier = pltpu.get_barrier_semaphore()
    for d in range(1, n_proj):
        pl.semaphore_signal(
            barrier, inc=1, device_id={"proj": lax.rem(z - d + n_proj, n_proj)}, device_id_type=MESH
        )
    for step in range(1, STEPS):
        source = lax.rem(here - step + n_train, n_train)
        pl.semaphore_signal(barrier, inc=1, device_id={"train": source}, device_id_type=MESH)
    pick_copy = pltpu.make_async_copy(pick_hbm, pick, small_sem.at[0])
    pick_copy.start()
    fisher_copy = pltpu.make_async_copy(fisher_hbm, fisher, small_sem.at[1])
    fisher_copy.start()
    pool_copies = []
    for c in range(NCHUNK):
        part = pl.ds(c * CHUNK, CHUNK)
        copy = pltpu.make_async_copy(pool_hbm.at[:, part], pools[c], pool_sem.at[c])
        copy.start()
        pool_copies.append(copy)
    train_copy = pltpu.make_async_copy(train_hbm, train, train_sem)
    train_copy.start()

    def far_copy(j, slot, p, cut):
        count, at = FAR_ROWS[p], FAR_AT[p]
        lanes = pl.ds(cut * (width // FAR_CUTS[p]), width // FAR_CUTS[p])
        return pltpu.make_async_remote_copy(
            src_ref=far_out.at[j, pl.ds(at, count), lanes],
            dst_ref=far_blocks[p].at[pl.ds(pl.multiple_of(slot * count, 16), count), lanes],
            send_sem=fsend_sem.at[j, p, cut],
            recv_sem=frecv_sem.at[slot, p, cut],
            device_id={"train": lax.rem(here + 2 - core + j, n_train)},
            device_id_type=MESH,
        )

    def near_copy(c):
        return pltpu.make_async_remote_copy(
            src_ref=near_out.at[pl.ds(c * CHUNK, CHUNK)],
            dst_ref=near_blocks[c].at[pl.ds(CHUNK, CHUNK)],
            send_sem=nsend_sem.at[c],
            recv_sem=nrecv_sem.at[c],
            device_id={"train": lax.rem(here + 1 + 2 * core, n_train)},
            device_id_type=MESH,
        )

    def condition(step, at, count, write):
        chosen = pick[step, here]
        piece = min(width, 512)
        c, first = at // CHUNK, at % CHUNK

        def body(i, _):
            part = pl.ds(pl.multiple_of(first + i * 16, 16), 16)
            for lane in range(0, width, piece):
                lanes = pl.ds(lane, piece)
                value = pools[c][chosen, part, lanes].astype(jnp.float32) * inv_root[:, lanes]
                write(pl.multiple_of(i * 16, 16), lanes, value.astype(jnp.bfloat16))
            return 0

        lax.fori_loop(0, count // 16, body, 0)

    pick_copy.wait()
    fisher_copy.wait()
    inv_root[...] = lax.rsqrt(fisher[...])
    entered = False
    for c in range(NCHUNK):
        pool_copies[c].wait()
        for p in range(NFAR):
            count, at = FAR_ROWS[p], FAR_AT[p]
            if at // CHUNK != c:
                continue
            for j in range(2):
                def write(i, lanes, value):
                    far_out[j, pl.ds(pl.multiple_of(at + i, 16), 16), lanes] = value

                condition(2 - core + j, at, count, write)
                if not entered:
                    pl.semaphore_wait(barrier, STEPS - 1 + n_proj - 1)
                    entered = True
                if FAR_CUTS[p] == 1:
                    far_copy(j, 1 - core, p, 0).start()
            if FAR_CUTS[p] > 1:
                for cut in range(FAR_CUTS[p]):
                    for j in range(2):
                        far_copy(j, 1 - core, p, cut).start()

        def write(i, lanes, value):
            near_out[pl.ds(pl.multiple_of(c * CHUNK + i, 16), 16), lanes] = value

        condition(1 + 2 * core, c * CHUNK, CHUNK, write)
        near_copy(c).start()
    for c in range(NCHUNK):
        def write(i, lanes, value):
            near_blocks[c][pl.ds(i, 16), lanes] = value

        condition(0, c * CHUNK, CHUNK, write)
    train_copy.wait()

    def partial_copy(k, d):
        to = lax.rem(z + d, n_proj)
        return pltpu.make_async_remote_copy(
            src_ref=partials[k].at[d - 1],
            dst_ref=landed[k].at[d - 1],
            send_sem=zsend_sem.at[k, d - 1],
            recv_sem=zrecv_sem.at[k, d - 1],
            device_id={"proj": to},
            device_id_type=MESH,
        )

    def finish(k, streams, count, at):
        fold = fold_of(count)
        share = owned // fold

        def add(d, total):
            partial_copy(k, d).wait_recv()
            return total + landed[k][d - 1].astype(jnp.float32)

        total = lax.fori_loop(1, n_proj, add, owns[k][...]) * scale
        for g in range(fold):
            for i, step in enumerate(streams):
                lane = g * 2 * count + i * count
                out[step, g * share:(g + 1) * share, at:at + count] = total[:, lane:lane + count]

    def dot(left, right):
        return lax.dot_general(left, right, (((1,), (1,)), ((), ())), preferred_element_type=jnp.float32)

    def mine(d):
        return pl.ds(pl.multiple_of(lax.rem(z + d, n_proj) * owned, 16), owned)

    near_in = 3 - 2 * core
    far_in = (1 + core, 2 + core)
    work = [((0, near_in), CHUNK, c * CHUNK, c, 1) for c in range(NCHUNK)]
    work += [(far_in, FAR_ROWS[p], FAR_AT[p], p, FAR_CUTS[p]) for p in range(NFAR)]
    for k, (streams, count, at, index, cuts) in enumerate(work):
        near = k < NCHUNK
        block = near_blocks[index] if near else far_blocks[index]
        fold = fold_of(count)
        share = owned // fold
        for cut in range(cuts):
            if near:
                near_copy(index).wait_recv()
            else:
                for slot in range(2):
                    far_copy(0, slot, index, cut).wait_recv()
            lanes = slice(cut * (width // cuts), (cut + 1) * (width // cuts))
            if cut < cuts - 1:
                def gather(d, _):
                    sums = dot(train[mine(d), lanes], block[:, lanes])
                    early[d - 1] = sums if cut == 0 else early[d - 1] + sums
                    return 0

                lax.fori_loop(1, n_proj + 1, gather, 0)
                continue

            def multiply(d, _):
                sums = dot(train[mine(d), lanes], block[:, lanes])
                if cuts > 1:
                    sums = sums + early[d - 1]
                if fold > 1:
                    sums = jnp.concatenate([sums[g * share:(g + 1) * share] for g in range(fold)], axis=1)

                @pl.when(d < n_proj)
                def _():
                    partials[k][d - 1] = sums.astype(jnp.bfloat16)
                    partial_copy(k, d).start()

                @pl.when(d == n_proj)
                def _():
                    owns[k][...] = sums

                return 0

            lax.fori_loop(1, n_proj + 1, multiply, 0)
        if k > 0:
            finish(k - 1, *work[k - 1][:3])
    finish(len(work) - 1, *work[-1][:3])

    for j in range(2):
        for p in range(NFAR):
            for cut in range(FAR_CUTS[p]):
                far_copy(j, 1 - core, p, cut).wait_send()
    for c in range(NCHUNK):
        near_copy(c).wait_send()
    for k in range(len(work)):
        def drain(d, _):
            partial_copy(k, d).wait_send()
            return 0

        lax.fori_loop(1, n_proj, drain, 0)


def on_device(n_train, n_proj, train_grads, queries, fisher, block_pick):
    rows, width = train_grads.shape
    owned = rows // n_proj
    counts = (CHUNK,) * NCHUNK + FAR_ROWS
    works = len(counts)
    bf16, f32 = jnp.bfloat16, jnp.float32
    dma = pltpu.SemaphoreType.DMA
    shares = [owned // fold_of(count) for count in counts]
    return pl.pallas_call(
        functools.partial(kernel, n_train, n_proj),
        out_shape=jax.ShapeDtypeStruct((STEPS, owned, QB), f32),
        in_specs=[pl.BlockSpec(memory_space=pl.ANY)] * 4,
        out_specs=pl.BlockSpec(memory_space=pltpu.VMEM),
        scratch_shapes=[
            pltpu.VMEM((rows, width), bf16),
            [pltpu.VMEM((QBLK, CHUNK, width), bf16)] * NCHUNK,
            pltpu.VMEM((1, width), f32),
            pltpu.VMEM((1, width), f32),
            pltpu.SMEM(block_pick.shape, jnp.int32),
            pltpu.VMEM((2, QB, width), bf16),
            pltpu.VMEM((QB, width), bf16),
            [pltpu.VMEM((2 * CHUNK, width), bf16)] * NCHUNK,
            [pltpu.VMEM((2 * count, width), bf16) for count in FAR_ROWS],
            [pltpu.VMEM((n_proj - 1, share, LANES), bf16) for share in shares],
            [pltpu.VMEM((share, LANES), f32) for share in shares],
            [pltpu.VMEM((n_proj - 1, share, LANES), bf16) for share in shares],
            pltpu.VMEM((n_proj, owned, 2 * FAR_ROWS[-1]), f32),
            dma(()),
            dma((NCHUNK,)),
            dma((2,)),
            dma((2, NFAR, MAX_CUTS)),
            dma((2, NFAR, MAX_CUTS)),
            dma((NCHUNK,)),
            dma((NCHUNK,)),
            dma((works, n_proj - 1)),
            dma((works, n_proj - 1)),
        ],
        compiler_params=pltpu.CompilerParams(
            collective_id=0, has_side_effects=True, vmem_limit_bytes=50 * 1024 * 1024
        ),
        cost_estimate=pl.CostEstimate(
            flops=2 * STEPS * rows * width * QB, bytes_accessed=2 * width * (rows + 512), transcendentals=width
        ),
    )(train_grads, queries.reshape(QBLK, QB, width), fisher.reshape(1, width), block_pick)


def solution(mesh):
    placed = (
        P(("groups", "train"), "proj"),
        P(("groups", "train"), "proj"),
        P(("groups", "proj")),
        P("groups", None),
    )
    return jax.shard_map(
        functools.partial(on_device, mesh.shape["train"], mesh.shape["proj"]),
        mesh=mesh,
        in_specs=placed,
        out_specs=P(None, ("groups", "train", "proj"), None),
        check_vma=False,
    )
```

```python
import functools

import jax
import jax.numpy as jnp
from jax import lax
from jax.experimental import pallas as pl
from jax.experimental.pallas import tpu as pltpu
from jax.sharding import PartitionSpec as P

P_SIZE = 16384
QB = 256
QBLK = 2
STEPS = 4
LANES = 128
CHUNK = 64
NCHUNK = QB // CHUNK
FAR_ROWS = (32, 32, 64, 64, 32, 16, 16)
FAR_AT = tuple(sum(FAR_ROWS[:i]) for i in range(len(FAR_ROWS)))
FAR_CUTS = (1,) * (len(FAR_ROWS) - 1) + (2,)
NFAR = len(FAR_ROWS)
MAX_CUTS = max(FAR_CUTS)
MESH = pl.DeviceIdType.MESH


def fold_of(count):
    return LANES // (2 * count)


def kernel(
    n_train, n_proj, train_hbm, pool_hbm, fisher_hbm, pick_hbm, out,
    train, pools, fisher, inv_root, pick, far_out, near_out, near_blocks, far_blocks,
    partials, owns, landed, early,
    inside, train_sem, pool_sem, small_sem, fsend_sem, frecv_sem, nsend_sem, nrecv_sem, zsend_sem, zrecv_sem,
):
    here, z = lax.axis_index("train"), lax.axis_index("proj")
    core = lax.rem(here, 2)
    rows, width = train.shape
    owned = rows // n_proj
    scale = P_SIZE ** (-0.5)

    barrier = pltpu.get_barrier_semaphore()
    for other in (z - 1, z + 1):
        @pl.when(jnp.logical_and(other >= 0, other < n_proj))
        def _():
            pl.semaphore_signal(barrier, inc=1, device_id={"proj": other}, device_id_type=MESH)

    for step in range(1, STEPS):
        source = lax.rem(here - step + n_train, n_train)
        pl.semaphore_signal(barrier, inc=1, device_id={"train": source}, device_id_type=MESH)
    beside = jnp.where(z > 0, 1, 0) + jnp.where(z < n_proj - 1, 1, 0)
    pick_copy = pltpu.make_async_copy(pick_hbm, pick, small_sem.at[0])
    pick_copy.start()
    fisher_copy = pltpu.make_async_copy(fisher_hbm, fisher, small_sem.at[1])
    fisher_copy.start()
    pool_copies = []
    for c in range(NCHUNK):
        part = pl.ds(c * CHUNK, CHUNK)
        copy = pltpu.make_async_copy(pool_hbm.at[:, part], pools[c], pool_sem.at[c])
        if c == 0:
            copy.start()
        pool_copies.append(copy)

    def far_copy(j, slot, p, cut):
        count, at = FAR_ROWS[p], FAR_AT[p]
        lanes = pl.ds(cut * (width // FAR_CUTS[p]), width // FAR_CUTS[p])
        return pltpu.make_async_remote_copy(
            src_ref=far_out.at[j, pl.ds(at, count), lanes],
            dst_ref=far_blocks[p].at[pl.ds(pl.multiple_of(slot * count, 16), count), lanes],
            send_sem=fsend_sem.at[j, p, cut],
            recv_sem=frecv_sem.at[slot, p, cut],
            device_id={"train": lax.rem(here + 2 - core + j, n_train)},
            device_id_type=MESH,
        )

    def near_copy(c):
        return pltpu.make_async_remote_copy(
            src_ref=near_out.at[pl.ds(c * CHUNK, CHUNK)],
            dst_ref=near_blocks[c].at[pl.ds(CHUNK, CHUNK)],
            send_sem=nsend_sem.at[c],
            recv_sem=nrecv_sem.at[c],
            device_id={"train": lax.rem(here + 1 + 2 * core, n_train)},
            device_id_type=MESH,
        )

    def condition(step, at, count, write):
        chosen = pick[step, here]
        piece = min(width, 512)
        c, first = at // CHUNK, at % CHUNK

        def body(i, _):
            part = pl.ds(pl.multiple_of(first + i * 16, 16), 16)
            for lane in range(0, width, piece):
                lanes = pl.ds(lane, piece)
                value = pools[c][chosen, part, lanes].astype(jnp.float32) * inv_root[:, lanes]
                write(pl.multiple_of(i * 16, 16), lanes, value.astype(jnp.bfloat16))
            return 0

        lax.fori_loop(0, count // 16, body, 0)

    pick_copy.wait()
    fisher_copy.wait()
    inv_root[...] = lax.rsqrt(fisher[...])
    entered = False
    for c in range(NCHUNK):
        pool_copies[c].wait()
        for p in range(NFAR):
            count, at = FAR_ROWS[p], FAR_AT[p]
            if at // CHUNK != c:
                continue
            for j in range(2):
                def write(i, lanes, value):
                    far_out[j, pl.ds(pl.multiple_of(at + i, 16), 16), lanes] = value

                condition(2 - core + j, at, count, write)
                if not entered:
                    pl.semaphore_wait(barrier, STEPS - 1 + beside)
                    entered = True
                if FAR_CUTS[p] == 1:
                    far_copy(j, 1 - core, p, 0).start()
            if FAR_CUTS[p] > 1:
                for cut in range(FAR_CUTS[p]):
                    for j in range(2):
                        far_copy(j, 1 - core, p, cut).start()

        def write(i, lanes, value):
            near_out[pl.ds(pl.multiple_of(c * CHUNK + i, 16), 16), lanes] = value

        if c == 0:
            for copy in pool_copies[1:]:
                copy.start()
        condition(1 + 2 * core, c * CHUNK, CHUNK, write)
        near_copy(c).start()
        if c == 0:
            train_copy = pltpu.make_async_copy(train_hbm, train, train_sem)
            train_copy.start()
    for c in range(NCHUNK):
        def write(i, lanes, value):
            near_blocks[c][pl.ds(i, 16), lanes] = value

        condition(0, c * CHUNK, CHUNK, write)
    train_copy.wait()

    def relay(i, _):
        for origin, onward in ((z - i, z + 1), (z + i, z - 1)):
            known = jnp.logical_and(origin >= 0, origin < n_proj)

            @pl.when(jnp.logical_and(known, i > 1))
            def _():
                pl.semaphore_wait(inside.at[origin], 1)

            @pl.when(jnp.logical_and(known, jnp.logical_and(onward >= 0, onward < n_proj)))
            def _():
                pl.semaphore_signal(
                    inside.at[origin], inc=1, device_id={"proj": onward}, device_id_type=MESH
                )
        return 0

    lax.fori_loop(1, n_proj, relay, 0)

    def partial_copy(k, d):
        to = lax.rem(z + d, n_proj)
        return pltpu.make_async_remote_copy(
            src_ref=partials[k].at[d - 1],
            dst_ref=landed[k].at[d - 1],
            send_sem=zsend_sem.at[k, d - 1],
            recv_sem=zrecv_sem.at[k, d - 1],
            device_id={"proj": to},
            device_id_type=MESH,
        )

    def finish(k, streams, count, at):
        fold = fold_of(count)
        share = owned // fold

        def add(d, total):
            partial_copy(k, d).wait_recv()
            return total + landed[k][d - 1].astype(jnp.float32)

        total = lax.fori_loop(1, n_proj, add, owns[k][...]) * scale
        for g in range(fold):
            for i, step in enumerate(streams):
                lane = g * 2 * count + i * count
                out[step, g * share:(g + 1) * share, at:at + count] = total[:, lane:lane + count]

    def dot(left, right):
        return lax.dot_general(left, right, (((1,), (1,)), ((), ())), preferred_element_type=jnp.float32)

    def mine(d):
        return pl.ds(pl.multiple_of(lax.rem(z + d, n_proj) * owned, 16), owned)

    def drain_far(p):
        for j in range(2):
            for cut in range(FAR_CUTS[p]):
                far_copy(j, 1 - core, p, cut).wait_send()

    def drain_partial(k):
        def drain(d, _):
            partial_copy(k, d).wait_send()
            return 0

        lax.fori_loop(1, n_proj, drain, 0)

    near_in = 3 - 2 * core
    far_in = (1 + core, 2 + core)
    work = [((0, near_in), CHUNK, c * CHUNK, c, 1) for c in range(NCHUNK)]
    work += [(far_in, FAR_ROWS[p], FAR_AT[p], p, FAR_CUTS[p]) for p in range(NFAR)]
    for k, (streams, count, at, index, cuts) in enumerate(work):
        near = k < NCHUNK
        block = near_blocks[index] if near else far_blocks[index]
        fold = fold_of(count)
        share = owned // fold
        for cut in range(cuts):
            if k > NCHUNK and cut == cuts - 1:
                finish(k - 1, *work[k - 1][:3])
            if k == len(work) - 1 and cut == cuts - 1:
                for p in range(NFAR - 1):
                    drain_far(p)
                for c in range(NCHUNK):
                    near_copy(c).wait_send()
                for before in range(k):
                    drain_partial(before)
            if near:
                near_copy(index).wait_recv()
            else:
                for slot in range(2):
                    far_copy(0, slot, index, cut).wait_recv()
            lanes = slice(cut * (width // cuts), (cut + 1) * (width // cuts))
            if cut < cuts - 1:
                def gather(d, _):
                    sums = dot(train[mine(d), lanes], block[:, lanes])
                    early[d - 1] = sums if cut == 0 else early[d - 1] + sums
                    return 0

                lax.fori_loop(1, n_proj + 1, gather, 0)
                continue

            def multiply(d, _):
                sums = dot(train[mine(d), lanes], block[:, lanes])
                if cuts > 1:
                    sums = sums + early[d - 1]
                if fold > 1:
                    sums = jnp.concatenate([sums[g * share:(g + 1) * share] for g in range(fold)], axis=1)

                @pl.when(d < n_proj)
                def _():
                    partials[k][d - 1] = sums.astype(jnp.bfloat16)
                    partial_copy(k, d).start()

                @pl.when(d == n_proj)
                def _():
                    owns[k][...] = sums

                return 0

            lax.fori_loop(1, n_proj + 1, multiply, 0)
        if 0 < k <= NCHUNK:
            finish(k - 1, *work[k - 1][:3])
    finish(len(work) - 1, *work[-1][:3])

    drain_far(NFAR - 1)
    drain_partial(len(work) - 1)


def on_device(n_train, n_proj, train_grads, queries, fisher, block_pick):
    rows, width = train_grads.shape
    owned = rows // n_proj
    counts = (CHUNK,) * NCHUNK + FAR_ROWS
    works = len(counts)
    bf16, f32 = jnp.bfloat16, jnp.float32
    dma = pltpu.SemaphoreType.DMA
    shares = [owned // fold_of(count) for count in counts]
    return pl.pallas_call(
        functools.partial(kernel, n_train, n_proj),
        out_shape=jax.ShapeDtypeStruct((STEPS, owned, QB), f32),
        in_specs=[pl.BlockSpec(memory_space=pl.ANY)] * 4,
        out_specs=pl.BlockSpec(memory_space=pltpu.VMEM),
        scratch_shapes=[
            pltpu.VMEM((rows, width), bf16),
            [pltpu.VMEM((QBLK, CHUNK, width), bf16)] * NCHUNK,
            pltpu.VMEM((1, width), f32),
            pltpu.VMEM((1, width), f32),
            pltpu.SMEM(block_pick.shape, jnp.int32),
            pltpu.VMEM((2, QB, width), bf16),
            pltpu.VMEM((QB, width), bf16),
            [pltpu.VMEM((2 * CHUNK, width), bf16)] * NCHUNK,
            [pltpu.VMEM((2 * count, width), bf16) for count in FAR_ROWS],
            [pltpu.VMEM((n_proj - 1, share, LANES), bf16) for share in shares],
            [pltpu.VMEM((share, LANES), f32) for share in shares],
            [pltpu.VMEM((n_proj - 1, share, LANES), bf16) for share in shares],
            pltpu.VMEM((n_proj, owned, 2 * FAR_ROWS[-1]), f32),
            pltpu.SemaphoreType.REGULAR((n_proj,)),
            dma(()),
            dma((NCHUNK,)),
            dma((2,)),
            dma((2, NFAR, MAX_CUTS)),
            dma((2, NFAR, MAX_CUTS)),
            dma((NCHUNK,)),
            dma((NCHUNK,)),
            dma((works, n_proj - 1)),
            dma((works, n_proj - 1)),
        ],
        compiler_params=pltpu.CompilerParams(
            collective_id=0, has_side_effects=True, vmem_limit_bytes=50 * 1024 * 1024
        ),
        cost_estimate=pl.CostEstimate(
            flops=2 * STEPS * rows * width * QB, bytes_accessed=2 * width * (rows + 512), transcendentals=width
        ),
    )(train_grads, queries.reshape(QBLK, QB, width), fisher.reshape(1, width), block_pick)


def solution(mesh):
    placed = (
        P(("groups", "train"), "proj"),
        P(("groups", "train"), "proj"),
        P(("groups", "proj")),
        P("groups", None),
    )
    return jax.shard_map(
        functools.partial(on_device, mesh.shape["train"], mesh.shape["proj"]),
        mesh=mesh,
        in_specs=placed,
        out_specs=P(None, ("groups", "train", "proj"), None),
        check_vma=False,
    )
```
